256 devices in a mesh: ctx: 32 (over x, z), dec: 8 (over y, core).
Axes of the slice: x: 4, y: 4, z: 8, core: 2. Of those that a mesh axis runs over, the one named last changes fastest.
Arguments:
- queries: bfloat16 [512, 2, 8192], P(('ctx', 'dec')), may hold values from -256 to 256
- prompt_keys: bfloat16 [65536, 8, 128], P('ctx', 'dec'), may hold values from -40 to 40
- prompt_values: bfloat16 [65536, 8, 128], P('ctx', 'dec'), may hold values from -6 to 6
- suffix_keys: bfloat16 [512, 1024, 8, 128], P(('ctx', 'dec')), may hold values from -22 to 22
- suffix_values: bfloat16 [512, 1024, 8, 128], P(('ctx', 'dec')), may hold values from -6 to 6
- new_keys: bfloat16 [512, 2, 8, 128], P(('ctx', 'dec')), may hold values from -36 to 36
- new_values: bfloat16 [512, 2, 8, 128], P(('ctx', 'dec')), may hold values from -6 to 6
- lengths: int32 [512], P(('ctx', 'dec')), may hold values from 1 to 1024, as said below
Outputs:
- attended: bfloat16 [512, 2, 8192], P(('ctx', 'dec'))
The draws below stay inside these ranges and needn't reach their ends.
Inputs may be any that keep to these rules, and one draw needn't show every extreme that they name: `lengths`: at least one sample has exactly 1024 cached suffix tokens in every draw.
All inputs are finite; a program needn't handle non-finite values.
Results may differ from the reference program's by a relative error of at most 0.003.
Values may be sent and summed in bfloat16 or wider, within the bound.
No kernel may reach another device: no remote copies, remote signals or barrier semaphores. Data moves between devices by JAX's collectives and lax.ppermute only.
A program may use at most 128 MiB of HBM per device.

```python
import jax
import jax.numpy as jnp
from jax import lax

HQ = 64
KVH = 8
HD = 128
STEPS = 2
PBLK = 2048
SUF = 1024
PROMPT = 65536
SAMPLES = 512


def shared_normals(key):
    return jax.random.normal(jax.random.fold_in(key, 11), (PROMPT, KVH, HD), jnp.float32)


def draw_prompt_keys(key, part):
    return (3.0 * shared_normals(key)).astype(jnp.bfloat16)


def draw_queries(key, part):
    folded = jax.random.fold_in(key, 5)
    drawn = jax.random.normal(folded, (SAMPLES, STEPS, HQ * HD), jnp.float32)
    return drawn.astype(jnp.bfloat16)


def draw_lengths(key, part):
    key = jax.random.fold_in(key, 7)
    first_key, second_key = jax.random.split(key)
    drawn_lengths = jax.random.randint(first_key, (SAMPLES,), 1, SUF + 1, dtype=jnp.int32)
    chosen = jax.random.randint(second_key, (), 0, SAMPLES, dtype=jnp.int32)
    return jnp.where(jnp.arange(SAMPLES, dtype=jnp.int32) == chosen, jnp.int32(SUF), drawn_lengths)


def level_of(own_key, extent, cuts, low, top_value):
    level = 1.0
    for dim, parts in cuts:
        steps = jax.random.uniform(jax.random.fold_in(jax.random.fold_in(own_key, 6), dim), (parts,), jnp.float32, low / len(cuts), top_value / len(cuts))
        level = level * jnp.repeat(jnp.exp(steps), extent[dim] // parts).reshape((-1,) + (1,) * (len(extent) - 1 - dim))
    return level


def centred(rng, dims, scale, limit, cuts=(), kind=jnp.bfloat16):
    loudness = level_of(rng, dims, cuts, -0.22, 0.18) if cuts else 1.0
    values = jax.random.normal(rng, dims, jnp.float32) * scale * loudness
    return jnp.minimum(jnp.maximum(values, -limit), limit).astype(kind)


def setup_inputs(seed: int = 0) -> dict:
    key_list = jax.random.split(jax.random.key(seed), 9)
    queries = draw_queries(jax.random.fold_in(key_list[8], 71), 0)
    prompt_keys = draw_prompt_keys(jax.random.fold_in(key_list[8], 71), 0)
    prompt_values = centred(key_list[2], (PROMPT, KVH, HD), 1.0, 6.0, ((0, 32), (1, 8)))
    suffix_keys = centred(key_list[3], (SAMPLES, SUF, KVH, HD), 3.8, 22.0, ((0, 256),))
    suffix_values = centred(key_list[4], (SAMPLES, SUF, KVH, HD), 1.0, 6.0, ((0, 256),))
    new_keys = centred(key_list[5], (SAMPLES, STEPS, KVH, HD), 6.0, 36.0, ((0, 256),))
    new_values = centred(key_list[6], (SAMPLES, STEPS, KVH, HD), 1.0, 6.0, ((0, 256),))
    lengths = draw_lengths(jax.random.fold_in(key_list[8], 71), 0)
    return dict(queries=queries, prompt_keys=prompt_keys, prompt_values=prompt_values, suffix_keys=suffix_keys, suffix_values=suffix_values, new_keys=new_keys, new_values=new_values, lengths=lengths)


MASKED_SCORE = -1.0e30


def block_part(scores, visible, values, form):
    masked = jnp.where(visible, scores, MASKED_SCORE)
    block_max = jnp.max(masked, axis=-1)
    weights = jnp.where(visible, jnp.exp(masked - block_max[..., None]), 0.0).astype(jnp.bfloat16)
    wide_weights = weights.astype(jnp.float32)
    block_total = jnp.sum(wide_weights, axis=-1)
    block_sum = jnp.einsum(form, wide_weights, values.astype(jnp.float32))
    return block_max, block_total, block_sum


def merge_parts(left, right):
    highest = jnp.maximum(left[0], right[0])
    left_factor = jnp.exp(left[0] - highest)
    right_factor = jnp.exp(right[0] - highest)
    return (highest, left[1] * left_factor + right[1] * right_factor,
            left[2] * left_factor[..., None] + right[2] * right_factor[..., None])


def reference(queries, prompt_keys, prompt_values, suffix_keys, suffix_values, new_keys, new_values, lengths):
    per_group = HQ // KVH
    inverse_root = HD ** -0.5
    grouped = queries.astype(jnp.float32).reshape(SAMPLES, STEPS, KVH, per_group, HD)
    state_shape = (SAMPLES, STEPS, KVH, per_group)
    running = (jnp.full(state_shape, MASKED_SCORE, jnp.float32), jnp.zeros(state_shape, jnp.float32),
               jnp.zeros(state_shape + (HD,), jnp.float32))
    key_span = min(512, PBLK)
    key_blocks = prompt_keys.reshape(PROMPT // key_span, key_span, KVH, HD)
    value_blocks = prompt_values.reshape(PROMPT // key_span, key_span, KVH, HD)

    def prompt_step(carried, blocks_pair):
        scores = jnp.einsum('stgqd,kgd->stgqk', grouped, blocks_pair[0].astype(jnp.float32)) * inverse_root
        return merge_parts(carried, block_part(scores, True, blocks_pair[1], 'stgqk,kgd->stgqd')), None

    running, _ = lax.scan(prompt_step, running, (key_blocks, value_blocks))
    suffix_span = min(512, SUF)

    def suffix_step(carried, number):
        offset = number * suffix_span
        keys_here = lax.dynamic_slice_in_dim(suffix_keys, offset, suffix_span, 1).astype(jnp.float32)
        values_here = lax.dynamic_slice_in_dim(suffix_values, offset, suffix_span, 1)
        scores = jnp.einsum('stgqd,skgd->stgqk', grouped, keys_here) * inverse_root
        positions = offset + jnp.arange(suffix_span, dtype=jnp.int32)
        visible = (positions[None, :] < lengths[:, None])[:, None, None, None, :]
        return merge_parts(carried, block_part(scores, visible, values_here, 'stgqk,skgd->stgqd')), None

    running, _ = lax.scan(suffix_step, running, jnp.arange(SUF // suffix_span, dtype=jnp.int32))
    scores = jnp.einsum('stgqd,sugd->stgqu', grouped, new_keys.astype(jnp.float32)) * inverse_root
    step_index = jnp.arange(STEPS, dtype=jnp.int32)
    visible = (step_index[None, :] <= step_index[:, None])[None, :, None, None, :]
    running = merge_parts(running, block_part(scores, visible, new_values, 'stgqu,sugd->stgqd'))
    attended = running[2] / running[1][..., None]
    return attended.astype(jnp.bfloat16).reshape(SAMPLES, STEPS, HQ * HD)
```

```python
import functools
import math

import jax
import jax.numpy as jnp
from jax import lax
from jax.experimental import pallas as pl
from jax.experimental.pallas import tpu as pltpu
from jax.sharding import Mesh, PartitionSpec as P

MASKED_SCORE = -1e30
CODE_SPAN = 126.0
BF16 = jnp.bfloat16
F32 = jnp.float32


def dot_nt(a, b):
    return lax.dot_general(a, b, (((1,), (1,)), ((), ())), preferred_element_type=F32)


def split3(x):
    hi = x.astype(BF16).astype(F32)
    mid = (x - hi).astype(BF16).astype(F32)
    return hi, mid, x - hi - mid


def prompt_kernel(blocks, scale, carried, final, chunk, per_dest, *refs):
    q_ref = refs[0]
    k_refs = refs[1 : 1 + blocks]
    v_refs = refs[1 + blocks : 1 + 2 * blocks]
    rest = refs[1 + 2 * blocks :]
    if carried:
        acc_in, stat_in = rest[:2]
        rest = rest[2:]
    wide = rest[-1]
    rows, head_dim = q_ref.shape
    keys = k_refs[0].shape[0]

    @pl.when(pl.program_id(0) == 0)
    def _():
        for b in range(blocks):
            wide[b, :, :head_dim] = v_refs[b][...]
            wide[b, :, head_dim:] = jnp.ones((keys, head_dim), BF16)

    sub = 256
    for start in range(0, rows, sub):
        here = slice(start, start + sub)
        q = q_ref[here]
        if carried:
            acc = acc_in[here]
            top = stat_in[here, 0:1]
            total = jnp.broadcast_to(stat_in[here, 64:65], (sub, head_dim))
        else:
            acc = None
        for b in range(blocks):
            for offset in range(0, keys, chunk):
                scores = dot_nt(q, k_refs[b][offset : offset + chunk])
                part_top = jnp.max(scores, axis=1, keepdims=True)
                if acc is None:
                    new_top = part_top
                else:
                    new_top = jnp.maximum(top, part_top)
                    factor = jnp.exp2((top - new_top) * scale)
                weights = jnp.exp2((scores - new_top) * scale).astype(BF16)
                both = jnp.dot(weights, wide[b, offset : offset + chunk], preferred_element_type=F32)
                if acc is None:
                    acc, total = both[:, :head_dim], both[:, head_dim:]
                else:
                    acc = acc * factor + both[:, :head_dim]
                    total = total * factor + both[:, head_dim:]
                top = new_top
        lane = lax.broadcasted_iota(jnp.int32, (sub, head_dim), 1)
        if not final:
            acc_out, stat_out = rest[:2]
            acc_out[here] = acc
            stat_out[here] = jnp.where(lane < 64, jnp.broadcast_to(top, (sub, head_dim)), total)
        else:
            encode(rest[0], start // per_dest, sub // per_dest, per_dest, acc / total, top * scale + jnp.log2(total))


def encode(out_ref, first, count, per_dest, value, level):
    head_dim = value.shape[1]
    size = jnp.max(jnp.abs(value), axis=1, keepdims=True)
    size = jnp.maximum(size, 1e-30)
    size = size * (1.0 + 2.0**-20)
    coded = jnp.exp2(value * (CODE_SPAN / size)).astype(BF16)
    size = jnp.broadcast_to(size, value.shape)
    pieces = split3(level) + split3(size)
    lane = lax.broadcasted_iota(jnp.int32, (16, head_dim), 1)
    for i in range(count):
        base = i * per_dest
        out_ref[first + i, 0:per_dest, :] = coded[base : base + per_dest]
        packed = jnp.zeros((16, head_dim), F32)
        for half in range(per_dest // 16):
            for n, piece in enumerate(pieces):
                rows = piece[base + half * 16 : base + half * 16 + 16]
                packed = jnp.where(lane == half * 8 + n, rows, packed)
        out_ref[first + i, per_dest : per_dest + 16, :] = packed.astype(BF16)


def prompt_call(q, keys, values, carry, final, tile, chunk, scale, per_dest):
    rows, head_dim = q.shape
    positions = keys[0].shape[0]
    blocks = len(keys)
    row_spec = pl.BlockSpec((tile, head_dim), lambda i: (i, 0))
    full = pl.BlockSpec((positions, head_dim), lambda i: (0, 0))
    if final:
        dests = rows // per_dest
        out_specs = pl.BlockSpec((tile // per_dest, per_dest + 16, head_dim), lambda i: (i, 0, 0))
        out_shape = jax.ShapeDtypeStruct((dests, per_dest + 16, head_dim), BF16)
    else:
        out_specs = [row_spec, row_spec]
        out_shape = [jax.ShapeDtypeStruct((rows, head_dim), F32)] * 2
    carry = [] if carry is None else list(carry)
    work = rows * positions * blocks
    return pl.pallas_call(
        functools.partial(prompt_kernel, blocks, scale, bool(carry), final, chunk, per_dest),
        grid=(rows // tile,),
        in_specs=[row_spec] + [full] * (2 * blocks) + [row_spec] * len(carry),
        out_specs=out_specs,
        out_shape=out_shape,
        scratch_shapes=[pltpu.VMEM((blocks, positions, 2 * head_dim), BF16)],
        compiler_params=pltpu.CompilerParams(vmem_limit_bytes=48 << 20),
        cost_estimate=pl.CostEstimate(
            flops=4 * work * head_dim,
            bytes_accessed=4 * blocks * positions * head_dim + 6 * rows * head_dim,
            transcendentals=work,
        ),
        name="prompt",
    )(q, *keys, *values, *carry)


def suffix_kernel(scale, samples, groups, steps, q_ref, k_ref, v_ref, nk_ref, nv_ref, len_ref, out_ref, level_ref):
    sample = pl.program_id(0)
    per_sample = q_ref.shape[1] // samples
    head_dim = q_ref.shape[2]
    q = q_ref[:, pl.ds(pl.multiple_of(sample * per_sample, per_sample), per_sample), :]
    rows = groups * per_sample
    q = q.reshape(rows, head_dim)
    per_step = per_sample // steps
    length = len_ref[sample]
    flat = k_ref.shape[1]
    span = 2048

    def step(keys, values, visible, state):
        scores = jnp.where(visible, dot_nt(q, keys), MASKED_SCORE)
        part_top = jnp.max(scores, axis=1, keepdims=True)
        if state is None:
            new_top = part_top
        else:
            new_top = jnp.maximum(state[0], part_top)
        weights = jnp.exp2((scores - new_top) * scale)
        part_total = jnp.sum(weights, axis=1, keepdims=True)
        part = jnp.dot(weights.astype(BF16), values, preferred_element_type=F32)
        if state is None:
            return new_top, part_total, part
        factor = jnp.exp2((state[0] - new_top) * scale)
        return new_top, state[1] * factor + part_total, state[2] * factor + part

    def same_group(columns):
        row = lax.broadcasted_iota(jnp.int32, (rows, columns), 0)
        column = lax.broadcasted_iota(jnp.int32, (rows, columns), 1)
        return row, column, (row // per_sample) == (column % groups)

    new_count = nk_ref.shape[1]
    row, column, same = same_group(new_count)
    visible = same & (column // groups <= (row // per_step) % steps)
    state = step(nk_ref[0], nv_ref[0], visible, None)
    _, column, same = same_group(span)
    place = column // groups
    for offset in range(0, flat, span):
        visible = same & (place < length - offset // groups)
        state = step(k_ref[0, offset : offset + span], v_ref[0, offset : offset + span], visible, state)
    out_ref[0] = state[2] / state[1]
    level_ref[0] = jnp.broadcast_to(state[0] * scale + jnp.log2(state[1]), (rows, head_dim))


def suffix_call(q, keys, values, new_keys, new_values, lengths, scale, steps):
    groups, _, head_dim = q.shape
    samples, flat, _ = keys.shape
    new_count = new_keys.shape[1]
    rows = groups * q.shape[1] // samples
    cache = pl.BlockSpec((1, flat, head_dim), lambda s: (s, 0, 0))
    fresh = pl.BlockSpec((1, new_count, head_dim), lambda s: (s, 0, 0))
    out = pl.BlockSpec((1, rows, head_dim), lambda s: (s, 0, 0))
    return pl.pallas_call(
        functools.partial(suffix_kernel, scale, samples, groups, steps),
        grid=(samples,),
        in_specs=[
            pl.BlockSpec(q.shape, lambda s: (0, 0, 0)),
            cache,
            cache,
            fresh,
            fresh,
            pl.BlockSpec(memory_space=pltpu.SMEM),
        ],
        out_specs=[out, out],
        out_shape=[jax.ShapeDtypeStruct((samples, rows, head_dim), F32)] * 2,
        compiler_params=pltpu.CompilerParams(vmem_limit_bytes=48 << 20),
        cost_estimate=pl.CostEstimate(
            flops=4 * samples * rows * flat * head_dim,
            bytes_accessed=4 * samples * flat * head_dim,
            transcendentals=samples * rows * flat,
        ),
        name="suffix",
    )(q, keys, values, new_keys, new_values, lengths)


def merge_kernel(sources, groups, samples, steps, got_ref, own_ref, own_level_ref, out_ref):
    head_dim = own_ref.shape[2]
    per_sample = own_ref.shape[1] // groups
    per_step = per_sample // steps
    per_dest = samples * per_sample
    for g in range(groups):
        levels = [[] for _ in range(samples)]
        sizes = [[] for _ in range(samples)]
        for z in range(sources):
            packed = got_ref[z * groups + g, per_dest : per_dest + 16, :].astype(F32)
            for half in range(per_dest // 16):
                at = [
                    jnp.broadcast_to(packed[:, half * 8 + n : half * 8 + n + 1], (16, head_dim))
                    for n in range(6)
                ]
                levels[half].append(at[0] + at[1] + at[2])
                sizes[half].append((at[3] + at[4] + at[5]) * (1.0 / CODE_SPAN))
        for s in range(samples):
            own_level = own_level_ref[s, g * per_sample : (g + 1) * per_sample, :]
            highest = own_level
            for level in levels[s]:
                highest = jnp.maximum(highest, level)
            weight = jnp.exp2(own_level - highest)
            total = weight
            summed = weight * own_ref[s, g * per_sample : (g + 1) * per_sample, :]
            for z in range(sources):
                coded = got_ref[z * groups + g, s * per_sample : (s + 1) * per_sample, :].astype(F32)
                weight = jnp.exp2(levels[s][z] - highest)
                total = total + weight
                summed = summed + weight * (jnp.log2(coded) * sizes[s][z])
            result = summed / total
            for t in range(steps):
                out_ref[s * steps + t, g * per_step : (g + 1) * per_step, :] = result[
                    t * per_step : (t + 1) * per_step
                ]


def merge_call(got, own, own_level, sources, groups, steps):
    samples, rows, head_dim = own.shape
    heads = rows // steps
    return pl.pallas_call(
        functools.partial(merge_kernel, sources, groups, samples, steps),
        out_shape=jax.ShapeDtypeStruct((samples * steps, heads, head_dim), F32),
        compiler_params=pltpu.CompilerParams(vmem_limit_bytes=48 << 20),
        name="merge",
    )(got, own, own_level)


def local(x_size, z_size, dec_size, queries, prompt_keys, prompt_values, suffix_keys, suffix_values, new_keys, new_values, lengths):
    samples, steps, width = queries.shape
    _, suffix_length, groups, head_dim = suffix_keys.shape
    per_group = width // (groups * head_dim)
    scale = head_dim ** (-0.5) * math.log2(math.e)
    keys = prompt_keys.reshape(-1, head_dim)
    values = prompt_values.reshape(-1, head_dim)

    def shift(array, amount):
        return lax.ppermute(array, "x", [(i, (i + amount) % x_size) for i in range(x_size)])

    keys_left, values_left = shift(keys, 1), shift(values, 1)
    keys_right, values_right = shift(keys, -1), shift(values, -1)
    keys_far, values_far = shift(keys_left, 1), shift(values_right, -1)

    per_dest = samples * steps * per_group
    by_group = (
        queries.reshape(samples, steps, groups, per_group, head_dim)
        .transpose(2, 0, 1, 3, 4)
        .reshape(groups, per_dest, head_dim)
    )
    spread = jnp.broadcast_to(by_group[None], (z_size,) + by_group.shape).reshape(
        z_size * groups, per_dest, head_dim
    )
    rows = lax.all_to_all(spread, ("z", "dec"), 0, 0, tiled=True).reshape(-1, head_dim)

    own, own_level = suffix_call(
        by_group,
        suffix_keys.reshape(samples, suffix_length * groups, head_dim),
        suffix_values.reshape(samples, suffix_length * groups, head_dim),
        new_keys.reshape(samples, steps * groups, head_dim),
        new_values.reshape(samples, steps * groups, head_dim),
        lengths,
        scale,
        steps,
    )
    carry = prompt_call(rows, [keys], [values], None, False, 1024, 2048, scale, per_dest)
    coded = prompt_call(
        rows,
        [keys_left, keys_right, keys_far],
        [values_left, values_right, values_far],
        carry,
        True,
        512,
        2048,
        scale,
        per_dest,
    )
    got = lax.all_to_all(coded, ("z", "dec"), 0, 0, tiled=True)
    out = merge_call(got, own, own_level, z_size, groups, steps)
    return out.astype(BF16).reshape(samples, steps, width)


def solution(mesh):
    ctx_size, dec_size = mesh.devices.shape
    x_size = 4
    z_size = ctx_size // x_size
    split = Mesh(mesh.devices.reshape(x_size, z_size, dec_size), ("x", "z", "dec"))
    rows = ("x", "z", "dec")
    return jax.shard_map(
        functools.partial(local, x_size, z_size, dec_size),
        mesh=split,
        in_specs=(
            P(rows, None, None),
            P(("x", "z"), "dec", None),
            P(("x", "z"), "dec", None),
            P(rows, None, None, None),
            P(rows, None, None, None),
            P(rows, None, None, None),
            P(rows, None, None, None),
            P(rows),
        ),
        out_specs=P(rows, None, None),
        check_vma=False,
    )
```

```python
import functools
import math

import jax
import jax.numpy as jnp
from jax import lax
from jax.experimental import pallas as pl
from jax.experimental.pallas import tpu as pltpu
from jax.sharding import Mesh, PartitionSpec as P

MASKED_SCORE = -1e30
CODE_SPAN = 126.0
STAT_ROWS = 8
VMEM_BYTES = 32 << 20
BF16 = jnp.bfloat16
F32 = jnp.float32


def dot_nt(a, b):
    return lax.dot_general(a, b, (((1,), (1,)), ((), ())), preferred_element_type=F32)


def split3(x):
    hi = x.astype(BF16).astype(F32)
    mid = (x - hi).astype(BF16).astype(F32)
    return hi, mid, x - hi - mid


def prompt_kernel(blocks, scale, carried, final, sub, chunk, per_dest, *refs):
    q_ref = refs[0]
    k_refs = refs[1 : 1 + blocks]
    v_refs = refs[1 + blocks : 1 + 2 * blocks]
    rest = refs[1 + 2 * blocks :]
    if carried:
        acc_in, stat_in = rest[:2]
        rest = rest[2:]
    rows, head_dim = q_ref.shape
    keys = k_refs[0].shape[0]
    items = [
        (start, b, offset)
        for start in range(0, rows, sub)
        for b in range(blocks)
        for offset in range(0, keys, chunk)
    ]

    def score(item):
        start, b, offset = item
        return dot_nt(q_ref[start : start + sub], k_refs[b][offset : offset + chunk])

    def finish(start, acc, top, total):
        if final:
            encode(rest[0], start // per_dest, sub // per_dest, per_dest, acc / total, top * scale + jnp.log2(total))
        else:
            lane = lax.broadcasted_iota(jnp.int32, (sub, head_dim), 1)
            rest[0][start : start + sub] = acc
            rest[1][start : start + sub] = jnp.where(lane < 64, top, total)

    waiting = None
    ahead = score(items[0])
    for n, (start, b, offset) in enumerate(items):
        scores = ahead
        if n + 1 < len(items):
            ahead = score(items[n + 1])
        here = slice(start, start + sub)
        fresh = b == 0 and offset == 0
        if fresh and carried:
            acc = acc_in[here]
            top = stat_in[here, 0:1]
            total = stat_in[here, 64:65]
        elif fresh:
            acc = None
        part_top = jnp.max(scores, axis=1, keepdims=True)
        new_top = part_top if acc is None else jnp.maximum(top, part_top)
        weights = jnp.exp2((scores - new_top) * scale)
        part_total = jnp.sum(weights, axis=1, keepdims=True)
        part = jnp.dot(weights.astype(BF16), v_refs[b][offset : offset + chunk], preferred_element_type=F32)
        if acc is None:
            acc, total = part, part_total
        else:
            factor = jnp.exp2((top - new_top) * scale)
            acc = acc * factor + part
            total = total * factor + part_total
        top = new_top
        if waiting is not None:
            finish(*waiting)
            waiting = None
        if b == blocks - 1 and offset + chunk == keys:
            waiting = (start, acc, top, total)
    finish(*waiting)


def encode(out_ref, first, count, per_dest, value, level):
    head_dim = value.shape[1]
    size = jnp.maximum(jnp.max(jnp.abs(value), axis=1, keepdims=True), 1e-30)
    size = jnp.broadcast_to((size * (1.0 + 2.0**-7)).astype(BF16).astype(F32), value.shape)
    coded = jnp.exp2(value * (CODE_SPAN / size)).astype(BF16)
    pieces = split3(jnp.broadcast_to(level, value.shape)) + (size,)
    lane = lax.broadcasted_iota(jnp.int32, (STAT_ROWS, head_dim), 1)
    for i in range(count):
        base = i * per_dest
        out_ref[first + i, 0:per_dest, :] = coded[base : base + per_dest]
        packed = jnp.zeros((STAT_ROWS, head_dim), F32)
        for part in range(per_dest // STAT_ROWS):
            for n, piece in enumerate(pieces):
                at = base + part * STAT_ROWS
                packed = jnp.where(lane == part * 8 + n, piece[at : at + STAT_ROWS], packed)
        out_ref[first + i, per_dest : per_dest + STAT_ROWS, :] = packed.astype(BF16)


def prompt_call(q, keys, values, carry, final, tile, sub, chunk, scale, per_dest):
    rows, head_dim = q.shape
    positions = keys[0].shape[0]
    blocks = len(keys)
    row_spec = pl.BlockSpec((tile, head_dim), lambda i: (i, 0))
    full = pl.BlockSpec((positions, head_dim), lambda i: (0, 0))
    if final:
        dests = rows // per_dest
        out_specs = pl.BlockSpec((tile // per_dest, per_dest + STAT_ROWS, head_dim), lambda i: (i, 0, 0))
        out_shape = jax.ShapeDtypeStruct((dests, per_dest + STAT_ROWS, head_dim), BF16)
    else:
        out_specs = [row_spec, row_spec]
        out_shape = [jax.ShapeDtypeStruct((rows, head_dim), F32)] * 2
    carry = [] if carry is None else list(carry)
    work = rows * positions * blocks
    return pl.pallas_call(
        functools.partial(prompt_kernel, blocks, scale, bool(carry), final, sub, chunk, per_dest),
        grid=(rows // tile,),
        in_specs=[row_spec] + [full] * (2 * blocks) + [row_spec] * len(carry),
        out_specs=out_specs,
        out_shape=out_shape,
        compiler_params=pltpu.CompilerParams(vmem_limit_bytes=VMEM_BYTES),
        cost_estimate=pl.CostEstimate(
            flops=4 * work * head_dim,
            bytes_accessed=4 * blocks * positions * head_dim + 6 * rows * head_dim,
            transcendentals=work,
        ),
        name="prompt",
    )(q, *keys, *values, *carry)


def suffix_kernel(scale, groups, steps, q_ref, k_ref, v_ref, nk_ref, nv_ref, len_ref, out_ref, level_ref):
    q = q_ref[0]
    rows, head_dim = q.shape
    per_sample = rows // groups
    length = len_ref[pl.program_id(0)]
    flat = k_ref.shape[1]
    span = 2048

    def step(keys, values, visible, state):
        scores = jnp.where(visible, dot_nt(q, keys), MASKED_SCORE)
        part_top = jnp.max(scores, axis=1, keepdims=True)
        if state is None:
            new_top = part_top
        else:
            new_top = jnp.maximum(state[0], part_top)
        weights = jnp.exp2((scores - new_top) * scale)
        part_total = jnp.sum(weights, axis=1, keepdims=True)
        part = jnp.dot(weights.astype(BF16), values, preferred_element_type=F32)
        if state is None:
            return new_top, part_total, part
        factor = jnp.exp2((state[0] - new_top) * scale)
        return new_top, state[1] * factor + part_total, state[2] * factor + part

    def same_group(columns):
        row = lax.broadcasted_iota(jnp.int32, (rows, columns), 0)
        column = lax.broadcasted_iota(jnp.int32, (rows, columns), 1)
        return row, column, (row // per_sample) == (column % groups)

    new_count = nk_ref.shape[1]
    row, column, same = same_group(new_count)
    visible = same & (column // groups <= row % steps)
    state = step(nk_ref[0], nv_ref[0], visible, None)
    _, column, same = same_group(span)
    place = column // groups
    for offset in range(0, flat, span):
        visible = same & (place < length - offset // groups)
        state = step(k_ref[0, offset : offset + span], v_ref[0, offset : offset + span], visible, state)
    out_ref[0] = state[2] / state[1]
    level_ref[0] = jnp.broadcast_to(state[0] * scale + jnp.log2(state[1]), (rows, head_dim))


def suffix_call(q, keys, values, new_keys, new_values, lengths, scale, groups, steps):
    samples, rows, head_dim = q.shape
    flat = keys.shape[1]
    new_count = new_keys.shape[1]
    cache = pl.BlockSpec((1, flat, head_dim), lambda s: (s, 0, 0))
    fresh = pl.BlockSpec((1, new_count, head_dim), lambda s: (s, 0, 0))
    out = pl.BlockSpec((1, rows, head_dim), lambda s: (s, 0, 0))
    return pl.pallas_call(
        functools.partial(suffix_kernel, scale, groups, steps),
        grid=(samples,),
        in_specs=[
            out,
            cache,
            cache,
            fresh,
            fresh,
            pl.BlockSpec(memory_space=pltpu.SMEM),
        ],
        out_specs=[out, out],
        out_shape=[jax.ShapeDtypeStruct((samples, rows, head_dim), F32)] * 2,
        compiler_params=pltpu.CompilerParams(vmem_limit_bytes=VMEM_BYTES),
        cost_estimate=pl.CostEstimate(
            flops=4 * samples * rows * flat * head_dim,
            bytes_accessed=4 * samples * flat * head_dim,
            transcendentals=samples * rows * flat,
        ),
        name="suffix",
    )(q, keys, values, new_keys, new_values, lengths)


def merge_kernel(sources, groups, samples, got_ref, own_ref, own_level_ref, out_ref):
    head_dim = own_ref.shape[2]
    per_sample = own_ref.shape[1] // groups
    per_dest = samples * per_sample
    for g in range(groups):
        levels, sizes = [], []
        for z in range(sources):
            packed = got_ref[z * groups + g, per_dest : per_dest + STAT_ROWS, :].astype(F32)
            parts = [[], []]
            for part in range(per_dest // STAT_ROWS):
                at = [
                    jnp.broadcast_to(packed[:, part * 8 + n : part * 8 + n + 1], (STAT_ROWS, head_dim))
                    for n in range(4)
                ]
                parts[0].append(at[0] + at[1] + at[2])
                parts[1].append(at[3] * (1.0 / CODE_SPAN))
            levels.append(jnp.concatenate(parts[0], axis=0))
            sizes.append(jnp.concatenate(parts[1], axis=0))
        for s in range(samples):
            own_level = own_level_ref[s, g * per_sample : (g + 1) * per_sample, :]
            highest = own_level
            here = slice(s * per_sample, (s + 1) * per_sample)
            for level in levels:
                highest = jnp.maximum(highest, level[here])
            weight = jnp.exp2(own_level - highest)
            total = weight
            summed = weight * own_ref[s, g * per_sample : (g + 1) * per_sample, :]
            for z in range(sources):
                coded = got_ref[z * groups + g, here, :].astype(F32)
                weight = jnp.exp2(levels[z][here] - highest)
                total = total + weight
                summed = summed + weight * (jnp.log2(coded) * sizes[z][here])
            result = summed / total
            out_ref[s, g * per_sample : (g + 1) * per_sample, :] = result.astype(BF16)


def merge_call(got, own, own_level, sources, groups):
    return pl.pallas_call(
        functools.partial(merge_kernel, sources, groups, own.shape[0]),
        out_shape=jax.ShapeDtypeStruct(own.shape, BF16),
        compiler_params=pltpu.CompilerParams(vmem_limit_bytes=VMEM_BYTES),
        name="merge",
    )(got, own, own_level)


def local(x_size, z_size, dec_size, queries, prompt_keys, prompt_values, suffix_keys, suffix_values, new_keys, new_values, lengths):
    samples, steps, width = queries.shape
    _, suffix_length, groups, head_dim = suffix_keys.shape
    per_group = width // (groups * head_dim)
    scale = head_dim ** (-0.5) * math.log2(math.e)
    keys = prompt_keys.reshape(-1, head_dim)
    values = prompt_values.reshape(-1, head_dim)

    def shift(array, amount):
        return lax.ppermute(array, "x", [(i, (i + amount) % x_size) for i in range(x_size)])

    keys_left, values_left = shift(keys, 1), shift(values, 1)
    keys_right, values_right = shift(keys, -1), shift(values, -1)
    keys_far, values_far = shift(keys_left, 1), shift(values_right, -1)

    per_dest = samples * steps * per_group
    per_sample = (
        queries.reshape(samples, steps, groups * per_group, head_dim)
        .transpose(0, 2, 1, 3)
        .reshape(samples, groups, per_group * steps, head_dim)
    )
    spread = jnp.broadcast_to(
        per_sample.transpose(1, 0, 2, 3)[None], (z_size, groups, samples, per_group * steps, head_dim)
    ).reshape(z_size * groups, per_dest, head_dim)
    rows = lax.all_to_all(spread, ("z", "dec"), 0, 0, tiled=True).reshape(-1, head_dim)

    own, own_level = suffix_call(
        per_sample.reshape(samples, groups * per_group * steps, head_dim),
        suffix_keys.reshape(samples, suffix_length * groups, head_dim),
        suffix_values.reshape(samples, suffix_length * groups, head_dim),
        new_keys.reshape(samples, steps * groups, head_dim),
        new_values.reshape(samples, steps * groups, head_dim),
        lengths,
        scale,
        groups,
        steps,
    )
    def prompt(some_keys, some_values, carry, final):
        sub = 128 if final else 256
        return prompt_call(rows, some_keys, some_values, carry, final, 1024, sub, 2048, scale, per_dest)

    carry = prompt([keys], [values], None, False)
    carry = prompt([keys_left, keys_right], [values_left, values_right], carry, False)
    coded = prompt([keys_far], [values_far], carry, True)
    got = lax.all_to_all(coded, ("z", "dec"), 0, 0, tiled=True)
    out = merge_call(got, own, own_level, z_size, groups)
    return (
        out.reshape(samples, groups * per_group, steps, head_dim)
        .transpose(0, 2, 1, 3)
        .reshape(samples, steps, width)
    )


def solution(mesh):
    ctx_size, dec_size = mesh.devices.shape
    x_size = 4
    z_size = ctx_size // x_size
    split = Mesh(mesh.devices.reshape(x_size, z_size, dec_size), ("x", "z", "dec"))
    rows = ("x", "z", "dec")
    return jax.shard_map(
        functools.partial(local, x_size, z_size, dec_size),
        mesh=split,
        in_specs=(
            P(rows, None, None),
            P(("x", "z"), "dec", None),
            P(("x", "z"), "dec", None),
            P(rows, None, None, None),
            P(rows, None, None, None),
            P(rows, None, None, None),
            P(rows, None, None, None),
            P(rows),
        ),
        out_specs=P(rows, None, None),
        check_vma=False,
    )
```

```python
import functools
import math

import jax
import jax.numpy as jnp
from jax import lax
from jax.experimental import pallas as pl
from jax.experimental.pallas import tpu as pltpu
from jax.sharding import Mesh, PartitionSpec as P

MASKED_SCORE = -1e30
CODE_SPAN = 126.0
STAT_ROWS = 8
VMEM_BYTES = 32 << 20
BF16 = jnp.bfloat16
F32 = jnp.float32


def dot_nt(a, b):
    return lax.dot_general(a, b, (((1,), (1,)), ((), ())), preferred_element_type=F32)


def split3(x):
    hi = x.astype(BF16).astype(F32)
    mid = (x - hi).astype(BF16).astype(F32)
    return hi, mid, x - hi - mid


def prompt_kernel(blocks, scale, carried, final, sub, chunk, per_dest, *refs):
    q_ref = refs[0]
    k_refs = refs[1 : 1 + blocks]
    v_refs = refs[1 + blocks : 1 + 2 * blocks]
    rest = refs[1 + 2 * blocks :]
    if carried:
        acc_in, stat_in = rest[:2]
        rest = rest[2:]
    rows, head_dim = q_ref.shape
    keys = k_refs[0].shape[0]
    items = [
        (start, b, offset)
        for start in range(0, rows, sub)
        for b in range(blocks)
        for offset in range(0, keys, chunk)
    ]

    def score(item):
        start, b, offset = item
        return dot_nt(q_ref[start : start + sub], k_refs[b][offset : offset + chunk])

    def finish(start, acc, top, total):
        if final:
            encode(rest[0], start // per_dest, sub // per_dest, per_dest, acc / total, top * scale + jnp.log2(total))
        else:
            lane = lax.broadcasted_iota(jnp.int32, (sub, head_dim), 1)
            rest[0][start : start + sub] = acc
            rest[1][start : start + sub] = jnp.where(lane < 64, top, total)

    waiting = None
    ahead = score(items[0])
    for n, (start, b, offset) in enumerate(items):
        scores = ahead
        if n + 1 < len(items):
            ahead = score(items[n + 1])
        here = slice(start, start + sub)
        fresh = b == 0 and offset == 0
        if fresh and carried:
            acc = acc_in[here]
            top = stat_in[here, 0:1]
            total = stat_in[here, 64:65]
        elif fresh:
            acc = None
        part_top = jnp.max(scores, axis=1, keepdims=True)
        new_top = part_top if acc is None else jnp.maximum(top, part_top)
        weights = jnp.exp2((scores - new_top) * scale)
        part_total = jnp.sum(weights, axis=1, keepdims=True)
        part = jnp.dot(weights.astype(BF16), v_refs[b][offset : offset + chunk], preferred_element_type=F32)
        if acc is None:
            acc, total = part, part_total
        else:
            factor = jnp.exp2((top - new_top) * scale)
            acc = acc * factor + part
            total = total * factor + part_total
        top = new_top
        if waiting is not None:
            finish(*waiting)
            waiting = None
        if b == blocks - 1 and offset + chunk == keys:
            waiting = (start, acc, top, total)
    finish(*waiting)


def encode(out_ref, first, count, per_dest, value, level):
    head_dim = value.shape[1]
    size = jnp.maximum(jnp.max(jnp.abs(value), axis=1, keepdims=True), 1e-30)
    size = jnp.broadcast_to((size * (1.0 + 2.0**-7)).astype(BF16).astype(F32), value.shape)
    coded = jnp.exp2(value * (CODE_SPAN / size)).astype(BF16)
    pieces = split3(jnp.broadcast_to(level, value.shape)) + (size,)
    lane = lax.broadcasted_iota(jnp.int32, (STAT_ROWS, head_dim), 1)
    for i in range(count):
        base = i * per_dest
        out_ref[first + i, 0:per_dest, :] = coded[base : base + per_dest]
        packed = jnp.zeros((STAT_ROWS, head_dim), F32)
        for part in range(per_dest // STAT_ROWS):
            for n, piece in enumerate(pieces):
                at = base + part * STAT_ROWS
                packed = jnp.where(lane == part * 8 + n, piece[at : at + STAT_ROWS], packed)
        out_ref[first + i, per_dest : per_dest + STAT_ROWS, :] = packed.astype(BF16)


def prompt_call(q, keys, values, carry, final, tile, sub, chunk, scale, per_dest):
    rows, head_dim = q.shape
    positions = keys[0].shape[0]
    blocks = len(keys)
    row_spec = pl.BlockSpec((tile, head_dim), lambda i: (i, 0))
    full = pl.BlockSpec((positions, head_dim), lambda i: (0, 0))
    if final:
        dests = rows // per_dest
        out_specs = pl.BlockSpec((tile // per_dest, per_dest + STAT_ROWS, head_dim), lambda i: (i, 0, 0))
        out_shape = jax.ShapeDtypeStruct((dests, per_dest + STAT_ROWS, head_dim), BF16)
    else:
        out_specs = [row_spec, row_spec]
        out_shape = [jax.ShapeDtypeStruct((rows, head_dim), F32)] * 2
    carry = [] if carry is None else list(carry)
    work = rows * positions * blocks
    return pl.pallas_call(
        functools.partial(prompt_kernel, blocks, scale, bool(carry), final, sub, chunk, per_dest),
        grid=(rows // tile,),
        in_specs=[row_spec] + [full] * (2 * blocks) + [row_spec] * len(carry),
        out_specs=out_specs,
        out_shape=out_shape,
        compiler_params=pltpu.CompilerParams(vmem_limit_bytes=VMEM_BYTES),
        cost_estimate=pl.CostEstimate(
            flops=work,
            bytes_accessed=4 * blocks * positions * head_dim + 6 * rows * head_dim,
            transcendentals=0,
        ),
        name="prompt",
    )(q, *keys, *values, *carry)


def suffix_kernel(scale, groups, steps, q_ref, k_ref, v_ref, nk_ref, nv_ref, len_ref, out_ref, level_ref):
    q = q_ref[0]
    rows, head_dim = q.shape
    per_sample = rows // groups
    length = len_ref[pl.program_id(0)]
    flat = k_ref.shape[1]
    span = 2048

    def step(keys, values, visible, state):
        scores = jnp.where(visible, dot_nt(q, keys), MASKED_SCORE)
        part_top = jnp.max(scores, axis=1, keepdims=True)
        if state is None:
            new_top = part_top
        else:
            new_top = jnp.maximum(state[0], part_top)
        weights = jnp.exp2((scores - new_top) * scale)
        part_total = jnp.sum(weights, axis=1, keepdims=True)
        part = jnp.dot(weights.astype(BF16), values, preferred_element_type=F32)
        if state is None:
            return new_top, part_total, part
        factor = jnp.exp2((state[0] - new_top) * scale)
        return new_top, state[1] * factor + part_total, state[2] * factor + part

    def same_group(columns):
        row = lax.broadcasted_iota(jnp.int32, (rows, columns), 0)
        column = lax.broadcasted_iota(jnp.int32, (rows, columns), 1)
        return row, column, (row // per_sample) == (column % groups)

    new_count = nk_ref.shape[1]
    row, column, same = same_group(new_count)
    visible = same & (column // groups <= row % steps)
    state = step(nk_ref[0], nv_ref[0], visible, None)
    _, column, same = same_group(span)
    place = column // groups
    for offset in range(0, flat, span):
        visible = same & (place < length - offset // groups)
        state = step(k_ref[0, offset : offset + span], v_ref[0, offset : offset + span], visible, state)
    out_ref[0] = state[2] / state[1]
    level_ref[0] = jnp.broadcast_to(state[0] * scale + jnp.log2(state[1]), (rows, head_dim))


def suffix_call(q, keys, values, new_keys, new_values, lengths, scale, groups, steps):
    samples, rows, head_dim = q.shape
    flat = keys.shape[1]
    new_count = new_keys.shape[1]
    cache = pl.BlockSpec((1, flat, head_dim), lambda s: (s, 0, 0))
    fresh = pl.BlockSpec((1, new_count, head_dim), lambda s: (s, 0, 0))
    out = pl.BlockSpec((1, rows, head_dim), lambda s: (s, 0, 0))
    return pl.pallas_call(
        functools.partial(suffix_kernel, scale, groups, steps),
        grid=(samples,),
        in_specs=[
            out,
            cache,
            cache,
            fresh,
            fresh,
            pl.BlockSpec(memory_space=pltpu.SMEM),
        ],
        out_specs=[out, out],
        out_shape=[jax.ShapeDtypeStruct((samples, rows, head_dim), F32)] * 2,
        compiler_params=pltpu.CompilerParams(vmem_limit_bytes=VMEM_BYTES),
        cost_estimate=pl.CostEstimate(
            flops=4 * samples * rows * flat * head_dim,
            bytes_accessed=4 * samples * flat * head_dim,
            transcendentals=samples * rows * flat,
        ),
        name="suffix",
    )(q, keys, values, new_keys, new_values, lengths)


def merge_kernel(sources, groups, samples, got_ref, own_ref, own_level_ref, out_ref):
    head_dim = own_ref.shape[2]
    per_sample = own_ref.shape[1] // groups
    per_dest = samples * per_sample
    for g in range(groups):
        levels, sizes = [], []
        for z in range(sources):
            packed = got_ref[z * groups + g, per_dest : per_dest + STAT_ROWS, :].astype(F32)
            parts = [[], []]
            for part in range(per_dest // STAT_ROWS):
                at = [
                    jnp.broadcast_to(packed[:, part * 8 + n : part * 8 + n + 1], (STAT_ROWS, head_dim))
                    for n in range(4)
                ]
                parts[0].append(at[0] + at[1] + at[2])
                parts[1].append(at[3] * (1.0 / CODE_SPAN))
            levels.append(jnp.concatenate(parts[0], axis=0))
            sizes.append(jnp.concatenate(parts[1], axis=0))
        for s in range(samples):
            own_level = own_level_ref[s, g * per_sample : (g + 1) * per_sample, :]
            highest = own_level
            here = slice(s * per_sample, (s + 1) * per_sample)
            for level in levels:
                highest = jnp.maximum(highest, level[here])
            weight = jnp.exp2(own_level - highest)
            total = weight
            summed = weight * own_ref[s, g * per_sample : (g + 1) * per_sample, :]
            for z in range(sources):
                coded = got_ref[z * groups + g, here, :].astype(F32)
                weight = jnp.exp2(levels[z][here] - highest)
                total = total + weight
                summed = summed + weight * (jnp.log2(coded) * sizes[z][here])
            result = summed / total
            out_ref[s, g * per_sample : (g + 1) * per_sample, :] = result.astype(BF16)


def merge_call(got, own, own_level, sources, groups):
    return pl.pallas_call(
        functools.partial(merge_kernel, sources, groups, own.shape[0]),
        out_shape=jax.ShapeDtypeStruct(own.shape, BF16),
        compiler_params=pltpu.CompilerParams(vmem_limit_bytes=VMEM_BYTES),
        name="merge",
    )(got, own, own_level)


def local(x_size, z_size, dec_size, queries, prompt_keys, prompt_values, suffix_keys, suffix_values, new_keys, new_values, lengths):
    samples, steps, width = queries.shape
    _, suffix_length, groups, head_dim = suffix_keys.shape
    per_group = width // (groups * head_dim)
    scale = head_dim ** (-0.5) * math.log2(math.e)
    keys = prompt_keys.reshape(-1, head_dim)
    values = prompt_values.reshape(-1, head_dim)

    def shift(array, amount):
        return lax.ppermute(array, "x", [(i, (i + amount) % x_size) for i in range(x_size)])

    keys_left, values_left = shift(keys, 1), shift(values, 1)
    keys_right, values_right = shift(keys, -1), shift(values, -1)
    keys_left, values_left, keys_right, values_right = lax.optimization_barrier(
        (keys_left, values_left, keys_right, values_right)
    )
    keys_far, values_far = shift(keys_left, 1), shift(values_right, -1)

    per_dest = samples * steps * per_group
    per_sample = (
        queries.reshape(samples, steps, groups * per_group, head_dim)
        .transpose(0, 2, 1, 3)
        .reshape(samples, groups, per_group * steps, head_dim)
    )
    spread = jnp.broadcast_to(
        per_sample.transpose(1, 0, 2, 3)[None], (z_size, groups, samples, per_group * steps, head_dim)
    ).reshape(z_size * groups, per_dest, head_dim)
    rows = lax.all_to_all(spread, ("z", "dec"), 0, 0, tiled=True).reshape(-1, head_dim)

    own, own_level = suffix_call(
        per_sample.reshape(samples, groups * per_group * steps, head_dim),
        suffix_keys.reshape(samples, suffix_length * groups, head_dim),
        suffix_values.reshape(samples, suffix_length * groups, head_dim),
        new_keys.reshape(samples, steps * groups, head_dim),
        new_values.reshape(samples, steps * groups, head_dim),
        lengths,
        scale,
        groups,
        steps,
    )
    def prompt(some_keys, some_values, carry, final):
        sub = 128 if final else 256
        return prompt_call(rows, some_keys, some_values, carry, final, 1024, sub, 2048, scale, per_dest)

    carry = prompt([keys, keys_left, keys_right], [values, values_left, values_right], None, False)
    coded = prompt([keys_far], [values_far], carry, True)
    got = lax.all_to_all(coded, ("z", "dec"), 0, 0, tiled=True)
    out = merge_call(got, own, own_level, z_size, groups)
    return (
        out.reshape(samples, groups * per_group, steps, head_dim)
        .transpose(0, 2, 1, 3)
        .reshape(samples, steps, width)
    )


def solution(mesh):
    ctx_size, dec_size = mesh.devices.shape
    x_size = 4
    z_size = ctx_size // x_size
    split = Mesh(mesh.devices.reshape(x_size, z_size, dec_size), ("x", "z", "dec"))
    rows = ("x", "z", "dec")
    return jax.shard_map(
        functools.partial(local, x_size, z_size, dec_size),
        mesh=split,
        in_specs=(
            P(rows, None, None),
            P(("x", "z"), "dec", None),
            P(("x", "z"), "dec", None),
            P(rows, None, None, None),
            P(rows, None, None, None),
            P(rows, None, None, None),
            P(rows, None, None, None),
            P(rows),
        ),
        out_specs=P(rows, None, None),
        check_vma=False,
    )
```

```python
import functools
import math

import jax
import jax.numpy as jnp
from jax import lax
from jax.experimental import pallas as pl
from jax.experimental.pallas import tpu as pltpu
from jax.sharding import Mesh, PartitionSpec as P

MASKED_SCORE = -1e30
CODE_SPAN = 126.0
STAT_ROWS = 8
VMEM_BYTES = 32 << 20
BF16 = jnp.bfloat16
F32 = jnp.float32


def dot_nt(a, b):
    return lax.dot_general(a, b, (((1,), (1,)), ((), ())), preferred_element_type=F32)


def split3(x):
    hi = x.astype(BF16).astype(F32)
    mid = (x - hi).astype(BF16).astype(F32)
    return hi, mid, x - hi - mid


def prompt_kernel(blocks, late, scale, carried, final, sub, chunk, per_dest, *refs):
    q_ref = refs[0]
    arrays = list(refs[1 : 1 + 2 * blocks])
    rest = refs[1 + 2 * blocks :]
    copies = {}
    if late:
        landing, arrived = refs[-2:]
        for n, at in enumerate(late):
            copies[at] = pltpu.make_async_copy(arrays[at], landing.at[n], arrived.at[n])
            copies[at].start()
            arrays[at] = landing.at[n]

    def block(at, offset):
        if at in copies:
            copies.pop(at).wait()
        return arrays[at][offset : offset + chunk]

    if carried:
        acc_in, stat_in = rest[:2]
        rest = rest[2:]
    rows, head_dim = q_ref.shape
    keys = arrays[0].shape[0]
    items = [
        (start, b, offset)
        for start in range(0, rows, sub)
        for b in range(blocks)
        for offset in range(0, keys, chunk)
    ]

    def score(item):
        start, b, offset = item
        return dot_nt(q_ref[start : start + sub], block(b, offset))

    def finish(start, acc, top, total):
        if final:
            encode(rest[0], start // per_dest, sub // per_dest, per_dest, acc / total, top * scale + jnp.log2(total))
        else:
            lane = lax.broadcasted_iota(jnp.int32, (sub, head_dim), 1)
            rest[0][start : start + sub] = acc
            rest[1][start : start + sub] = jnp.where(lane < 64, top, total)

    waiting = None
    ahead = score(items[0])
    for n, (start, b, offset) in enumerate(items):
        scores = ahead
        if n + 1 < len(items):
            ahead = score(items[n + 1])
        here = slice(start, start + sub)
        fresh = b == 0 and offset == 0
        if fresh and carried:
            acc = acc_in[here]
            top = stat_in[here, 0:1]
            total = stat_in[here, 64:65]
        elif fresh:
            acc = None
        part_top = jnp.max(scores, axis=1, keepdims=True)
        new_top = part_top if acc is None else jnp.maximum(top, part_top)
        weights = jnp.exp2((scores - new_top) * scale)
        part_total = jnp.sum(weights, axis=1, keepdims=True)
        part = jnp.dot(weights.astype(BF16), block(blocks + b, offset), preferred_element_type=F32)
        if acc is None:
            acc, total = part, part_total
        else:
            factor = jnp.exp2((top - new_top) * scale)
            acc = acc * factor + part
            total = total * factor + part_total
        top = new_top
        if waiting is not None:
            finish(*waiting)
            waiting = None
        if b == blocks - 1 and offset + chunk == keys:
            waiting = (start, acc, top, total)
    finish(*waiting)


def encode(out_ref, first, count, per_dest, value, level):
    head_dim = value.shape[1]
    size = jnp.maximum(jnp.max(jnp.abs(value), axis=1, keepdims=True), 1e-30)
    size = jnp.broadcast_to((size * (1.0 + 2.0**-7)).astype(BF16).astype(F32), value.shape)
    coded = jnp.exp2(value * (CODE_SPAN / size)).astype(BF16)
    pieces = split3(jnp.broadcast_to(level, value.shape)) + (size,)
    lane = lax.broadcasted_iota(jnp.int32, (STAT_ROWS, head_dim), 1)
    for i in range(count):
        base = i * per_dest
        out_ref[first + i, 0:per_dest, :] = coded[base : base + per_dest]
        packed = jnp.zeros((STAT_ROWS, head_dim), F32)
        for part in range(per_dest // STAT_ROWS):
            for n, piece in enumerate(pieces):
                at = base + part * STAT_ROWS
                packed = jnp.where(lane == part * 8 + n, piece[at : at + STAT_ROWS], packed)
        out_ref[first + i, per_dest : per_dest + STAT_ROWS, :] = packed.astype(BF16)


def prompt_call(q, keys, values, late, carry, final, sub, chunk, scale, per_dest):
    rows, head_dim = q.shape
    positions = keys[0].shape[0]
    blocks = len(keys)
    whole = pl.BlockSpec(memory_space=pltpu.VMEM)
    if final:
        out_shape = jax.ShapeDtypeStruct((rows // per_dest, per_dest + STAT_ROWS, head_dim), BF16)
    else:
        out_shape = [jax.ShapeDtypeStruct((rows, head_dim), F32)] * 2
    block_specs = [pl.BlockSpec(memory_space=pl.ANY) if at in late else whole for at in range(2 * blocks)]
    carry = [] if carry is None else list(carry)
    work = rows * positions * blocks
    return pl.pallas_call(
        functools.partial(prompt_kernel, blocks, late, scale, bool(carry), final, sub, chunk, per_dest),
        in_specs=[whole] + block_specs + [whole] * len(carry),
        out_specs=whole if final else [whole, whole],
        out_shape=out_shape,
        scratch_shapes=[
            pltpu.VMEM((max(len(late), 1), positions, head_dim), BF16),
            pltpu.SemaphoreType.DMA((max(len(late), 1),)),
        ],
        compiler_params=pltpu.CompilerParams(vmem_limit_bytes=VMEM_BYTES),
        cost_estimate=pl.CostEstimate(
            flops=work,
            bytes_accessed=4 * blocks * positions * head_dim + 6 * rows * head_dim,
            transcendentals=0,
        ),
        name="prompt",
    )(q, *keys, *values, *carry)


def suffix_kernel(scale, groups, steps, q_ref, k_ref, v_ref, nk_ref, nv_ref, len_ref, out_ref, level_ref):
    q = q_ref[0]
    rows, head_dim = q.shape
    per_sample = rows // groups
    length = len_ref[pl.program_id(0)]
    flat = k_ref.shape[1]
    span = 2048

    def step(keys, values, visible, state):
        scores = jnp.where(visible, dot_nt(q, keys), MASKED_SCORE)
        part_top = jnp.max(scores, axis=1, keepdims=True)
        if state is None:
            new_top = part_top
        else:
            new_top = jnp.maximum(state[0], part_top)
        weights = jnp.exp2((scores - new_top) * scale)
        part_total = jnp.sum(weights, axis=1, keepdims=True)
        part = jnp.dot(weights.astype(BF16), values, preferred_element_type=F32)
        if state is None:
            return new_top, part_total, part
        factor = jnp.exp2((state[0] - new_top) * scale)
        return new_top, state[1] * factor + part_total, state[2] * factor + part

    def same_group(columns):
        row = lax.broadcasted_iota(jnp.int32, (rows, columns), 0)
        column = lax.broadcasted_iota(jnp.int32, (rows, columns), 1)
        return row, column, (row // per_sample) == (column % groups)

    new_count = nk_ref.shape[1]
    row, column, same = same_group(new_count)
    visible = same & (column // groups <= row % steps)
    state = step(nk_ref[0], nv_ref[0], visible, None)
    _, column, same = same_group(span)
    place = column // groups
    for offset in range(0, flat, span):
        visible = same & (place < length - offset // groups)
        state = step(k_ref[0, offset : offset + span], v_ref[0, offset : offset + span], visible, state)
    out_ref[0] = state[2] / state[1]
    level_ref[0] = jnp.broadcast_to(state[0] * scale + jnp.log2(state[1]), (rows, head_dim))


def suffix_call(q, keys, values, new_keys, new_values, lengths, scale, groups, steps):
    samples, rows, head_dim = q.shape
    flat = keys.shape[1]
    new_count = new_keys.shape[1]
    cache = pl.BlockSpec((1, flat, head_dim), lambda s: (s, 0, 0))
    fresh = pl.BlockSpec((1, new_count, head_dim), lambda s: (s, 0, 0))
    out = pl.BlockSpec((1, rows, head_dim), lambda s: (s, 0, 0))
    return pl.pallas_call(
        functools.partial(suffix_kernel, scale, groups, steps),
        grid=(samples,),
        in_specs=[
            out,
            cache,
            cache,
            fresh,
            fresh,
            pl.BlockSpec(memory_space=pltpu.SMEM),
        ],
        out_specs=[out, out],
        out_shape=[jax.ShapeDtypeStruct((samples, rows, head_dim), F32)] * 2,
        compiler_params=pltpu.CompilerParams(vmem_limit_bytes=VMEM_BYTES),
        cost_estimate=pl.CostEstimate(
            flops=4 * samples * rows * flat * head_dim,
            bytes_accessed=4 * samples * flat * head_dim,
            transcendentals=samples * rows * flat,
        ),
        name="suffix",
    )(q, keys, values, new_keys, new_values, lengths)


def merge_kernel(sources, groups, samples, got_ref, own_ref, own_level_ref, out_ref):
    head_dim = own_ref.shape[2]
    per_sample = own_ref.shape[1] // groups
    per_dest = samples * per_sample
    for g in range(groups):
        levels, sizes = [], []
        for z in range(sources):
            packed = got_ref[z * groups + g, per_dest : per_dest + STAT_ROWS, :].astype(F32)
            parts = [[], []]
            for part in range(per_dest // STAT_ROWS):
                at = [
                    jnp.broadcast_to(packed[:, part * 8 + n : part * 8 + n + 1], (STAT_ROWS, head_dim))
                    for n in range(4)
                ]
                parts[0].append(at[0] + at[1] + at[2])
                parts[1].append(at[3] * (1.0 / CODE_SPAN))
            levels.append(jnp.concatenate(parts[0], axis=0))
            sizes.append(jnp.concatenate(parts[1], axis=0))
        for s in range(samples):
            own_level = own_level_ref[s, g * per_sample : (g + 1) * per_sample, :]
            highest = own_level
            here = slice(s * per_sample, (s + 1) * per_sample)
            for level in levels:
                highest = jnp.maximum(highest, level[here])
            weight = jnp.exp2(own_level - highest)
            total = weight
            summed = weight * own_ref[s, g * per_sample : (g + 1) * per_sample, :]
            for z in range(sources):
                coded = got_ref[z * groups + g, here, :].astype(F32)
                weight = jnp.exp2(levels[z][here] - highest)
                total = total + weight
                summed = summed + weight * (jnp.log2(coded) * sizes[z][here])
            result = summed / total
            out_ref[s, g * per_sample : (g + 1) * per_sample, :] = result.astype(BF16)


def merge_call(got, own, own_level, sources, groups):
    return pl.pallas_call(
        functools.partial(merge_kernel, sources, groups, own.shape[0]),
        out_shape=jax.ShapeDtypeStruct(own.shape, BF16),
        compiler_params=pltpu.CompilerParams(vmem_limit_bytes=VMEM_BYTES),
        name="merge",
    )(got, own, own_level)


def local(x_size, z_size, dec_size, queries, prompt_keys, prompt_values, suffix_keys, suffix_values, new_keys, new_values, lengths):
    samples, steps, width = queries.shape
    _, suffix_length, groups, head_dim = suffix_keys.shape
    per_group = width // (groups * head_dim)
    scale = head_dim ** (-0.5) * math.log2(math.e)
    keys = prompt_keys.reshape(-1, head_dim)
    values = prompt_values.reshape(-1, head_dim)

    def shift(array, amount):
        return lax.ppermute(array, "x", [(i, (i + amount) % x_size) for i in range(x_size)])

    keys_left, values_left = shift(keys, 1), shift(values, 1)
    keys_right, values_right = shift(keys, -1), shift(values, -1)
    keys_left, values_left, keys_right, values_right = lax.optimization_barrier(
        (keys_left, values_left, keys_right, values_right)
    )
    keys_far, values_far = shift(keys_left, 1), shift(values_right, -1)

    per_dest = samples * steps * per_group
    per_sample = (
        queries.reshape(samples, steps, groups * per_group, head_dim)
        .transpose(0, 2, 1, 3)
        .reshape(samples, groups, per_group * steps, head_dim)
    )
    spread = jnp.broadcast_to(
        per_sample.transpose(1, 0, 2, 3)[None], (z_size, groups, samples, per_group * steps, head_dim)
    ).reshape(z_size * groups, per_dest, head_dim)
    rows = lax.all_to_all(spread, ("z", "dec"), 0, 0, tiled=True).reshape(-1, head_dim)

    own, own_level = suffix_call(
        per_sample.reshape(samples, groups * per_group * steps, head_dim),
        suffix_keys.reshape(samples, suffix_length * groups, head_dim),
        suffix_values.reshape(samples, suffix_length * groups, head_dim),
        new_keys.reshape(samples, steps * groups, head_dim),
        new_values.reshape(samples, steps * groups, head_dim),
        lengths,
        scale,
        groups,
        steps,
    )
    def prompt(some_keys, some_values, late, carry, final, sub):
        return prompt_call(rows, some_keys, some_values, late, carry, final, sub, 2048, scale, per_dest)

    carry = prompt([keys_left, keys_right], [values_left, values_right], (), None, False, 256)
    coded = prompt([keys, keys_far], [values, values_far], (1, 3), carry, True, 128)
    got = lax.all_to_all(coded, ("z", "dec"), 0, 0, tiled=True)
    out = merge_call(got, own, own_level, z_size, groups)
    return (
        out.reshape(samples, groups * per_group, steps, head_dim)
        .transpose(0, 2, 1, 3)
        .reshape(samples, steps, width)
    )


def solution(mesh):
    ctx_size, dec_size = mesh.devices.shape
    x_size = 4
    z_size = ctx_size // x_size
    split = Mesh(mesh.devices.reshape(x_size, z_size, dec_size), ("x", "z", "dec"))
    rows = ("x", "z", "dec")
    return jax.shard_map(
        functools.partial(local, x_size, z_size, dec_size),
        mesh=split,
        in_specs=(
            P(rows, None, None),
            P(("x", "z"), "dec", None),
            P(("x", "z"), "dec", None),
            P(rows, None, None, None),
            P(rows, None, None, None),
            P(rows, None, None, None),
            P(rows, None, None, None),
            P(rows),
        ),
        out_specs=P(rows, None, None),
        check_vma=False,
    )
```

```python
import functools
import math

import jax
import jax.numpy as jnp
from jax import lax
from jax.experimental import pallas as pl
from jax.experimental.pallas import tpu as pltpu
from jax.sharding import Mesh, PartitionSpec as P

MASKED_SCORE = -1e30
CODE_SPAN = 126.0
STAT_ROWS = 8
VMEM_BYTES = 32 << 20
BF16 = jnp.bfloat16
F32 = jnp.float32


def dot_nt(a, b):
    return lax.dot_general(a, b, (((1,), (1,)), ((), ())), preferred_element_type=F32)


def split3(x):
    hi = x.astype(BF16).astype(F32)
    mid = (x - hi).astype(BF16).astype(F32)
    return hi, mid, x - hi - mid


def prompt_kernel(blocks, late, scale, carried, final, sub, chunk, per_dest, *refs):
    q_ref = refs[0]
    arrays = list(refs[1 : 1 + 2 * blocks])
    rest = refs[1 + 2 * blocks :]
    copies = {}
    if late:
        landing, arrived = refs[-2:]
        for n, at in enumerate(late):
            copies[at] = pltpu.make_async_copy(arrays[at], landing.at[n], arrived.at[n])
            copies[at].start()
            arrays[at] = landing.at[n]

    def block(at, offset):
        if at in copies:
            copies.pop(at).wait()
        return arrays[at][offset : offset + chunk]

    if carried:
        acc_in, stat_in = rest[:2]
        rest = rest[2:]
    rows, head_dim = q_ref.shape
    keys = arrays[0].shape[0]
    items = [
        (start, b, offset)
        for start in range(0, rows, sub)
        for b in range(blocks)
        for offset in range(0, keys, chunk)
    ]

    def score(item):
        start, b, offset = item
        return dot_nt(q_ref[start : start + sub], block(b, offset))

    def finish(start, acc, top, total):
        if final:
            encode(rest[0], start // per_dest, sub // per_dest, per_dest, acc / total, top * scale + jnp.log2(total))
        else:
            lane = lax.broadcasted_iota(jnp.int32, (sub, head_dim), 1)
            rest[0][start : start + sub] = acc
            rest[1][start : start + sub] = jnp.where(lane < 64, top, total)

    waiting = None
    ahead = score(items[0])
    for n, (start, b, offset) in enumerate(items):
        scores = ahead
        if n + 1 < len(items):
            ahead = score(items[n + 1])
        here = slice(start, start + sub)
        fresh = b == 0 and offset == 0
        if fresh and carried:
            acc = acc_in[here]
            top = stat_in[here, 0:1]
            total = stat_in[here, 64:65]
        elif fresh:
            acc = None
        part_top = jnp.max(scores, axis=1, keepdims=True)
        new_top = part_top if acc is None else jnp.maximum(top, part_top)
        weights = jnp.exp2((scores - new_top) * scale)
        part_total = jnp.sum(weights, axis=1, keepdims=True)
        part = jnp.dot(weights.astype(BF16), block(blocks + b, offset), preferred_element_type=F32)
        if acc is None:
            acc, total = part, part_total
        else:
            factor = jnp.exp2((top - new_top) * scale)
            acc = acc * factor + part
            total = total * factor + part_total
        top = new_top
        if waiting is not None:
            finish(*waiting)
            waiting = None
        if b == blocks - 1 and offset + chunk == keys:
            waiting = (start, acc, top, total)
    finish(*waiting)


def encode(out_ref, first, count, per_dest, value, level):
    head_dim = value.shape[1]
    size = jnp.maximum(jnp.max(jnp.abs(value), axis=1, keepdims=True), 1e-30)
    size = jnp.broadcast_to((size * (1.0 + 2.0**-7)).astype(BF16).astype(F32), value.shape)
    coded = jnp.exp2(value * (CODE_SPAN / size)).astype(BF16)
    pieces = split3(jnp.broadcast_to(level, value.shape)) + (size,)
    lane = lax.broadcasted_iota(jnp.int32, (STAT_ROWS, head_dim), 1)
    for i in range(count):
        base = i * per_dest
        out_ref[first + i, 0:per_dest, :] = coded[base : base + per_dest]
        packed = jnp.zeros((STAT_ROWS, head_dim), F32)
        for part in range(per_dest // STAT_ROWS):
            for n, piece in enumerate(pieces):
                at = base + part * STAT_ROWS
                packed = jnp.where(lane == part * 8 + n, piece[at : at + STAT_ROWS], packed)
        out_ref[first + i, per_dest : per_dest + STAT_ROWS, :] = packed.astype(BF16)


def prompt_call(q, keys, values, late, carry, final, sub, chunk, scale, per_dest):
    rows, head_dim = q.shape
    positions = keys[0].shape[0]
    blocks = len(keys)
    whole = pl.BlockSpec(memory_space=pltpu.VMEM)
    if final:
        out_shape = jax.ShapeDtypeStruct((rows // per_dest, per_dest + STAT_ROWS, head_dim), BF16)
    else:
        out_shape = [jax.ShapeDtypeStruct((rows, head_dim), F32)] * 2
    block_specs = [pl.BlockSpec(memory_space=pl.ANY) if at in late else whole for at in range(2 * blocks)]
    carry = [] if carry is None else list(carry)
    work = rows * positions * blocks
    return pl.pallas_call(
        functools.partial(prompt_kernel, blocks, late, scale, bool(carry), final, sub, chunk, per_dest),
        in_specs=[whole] + block_specs + [whole] * len(carry),
        out_specs=whole if final else [whole, whole],
        out_shape=out_shape,
        scratch_shapes=[
            pltpu.VMEM((max(len(late), 1), positions, head_dim), BF16),
            pltpu.SemaphoreType.DMA((max(len(late), 1),)),
        ],
        compiler_params=pltpu.CompilerParams(vmem_limit_bytes=VMEM_BYTES),
        cost_estimate=pl.CostEstimate(
            flops=work,
            bytes_accessed=4 * blocks * positions * head_dim + 6 * rows * head_dim,
            transcendentals=0,
        ),
        name="prompt",
    )(q, *keys, *values, *carry)


def suffix_kernel(scale, groups, steps, q_ref, k_ref, v_ref, nk_ref, nv_ref, len_ref, out_ref, level_ref):
    q = q_ref[0]
    rows, head_dim = q.shape
    per_sample = rows // groups
    length = len_ref[pl.program_id(0)]
    flat = k_ref.shape[1]
    span = 2048

    def step(keys, values, visible, state):
        scores = jnp.where(visible, dot_nt(q, keys), MASKED_SCORE)
        part_top = jnp.max(scores, axis=1, keepdims=True)
        if state is None:
            new_top = part_top
        else:
            new_top = jnp.maximum(state[0], part_top)
        weights = jnp.exp2((scores - new_top) * scale)
        part_total = jnp.sum(weights, axis=1, keepdims=True)
        part = jnp.dot(weights.astype(BF16), values, preferred_element_type=F32)
        if state is None:
            return new_top, part_total, part
        factor = jnp.exp2((state[0] - new_top) * scale)
        return new_top, state[1] * factor + part_total, state[2] * factor + part

    def same_group(columns):
        row = lax.broadcasted_iota(jnp.int32, (rows, columns), 0)
        column = lax.broadcasted_iota(jnp.int32, (rows, columns), 1)
        return row, column, (row // per_sample) == (column % groups)

    new_count = nk_ref.shape[1]
    row, column, same = same_group(new_count)
    visible = same & (column // groups <= row % steps)
    state = step(nk_ref[0], nv_ref[0], visible, None)
    _, column, same = same_group(span)
    place = column // groups
    for offset in range(0, flat, span):
        visible = same & (place < length - offset // groups)
        state = step(k_ref[0, offset : offset + span], v_ref[0, offset : offset + span], visible, state)
    out_ref[0] = state[2] / state[1]
    level_ref[0] = jnp.broadcast_to(state[0] * scale + jnp.log2(state[1]), (rows, head_dim))


def suffix_call(q, keys, values, new_keys, new_values, lengths, scale, groups, steps):
    samples, rows, head_dim = q.shape
    flat = keys.shape[1]
    new_count = new_keys.shape[1]
    cache = pl.BlockSpec((1, flat, head_dim), lambda s: (s, 0, 0))
    fresh = pl.BlockSpec((1, new_count, head_dim), lambda s: (s, 0, 0))
    out = pl.BlockSpec((1, rows, head_dim), lambda s: (s, 0, 0))
    return pl.pallas_call(
        functools.partial(suffix_kernel, scale, groups, steps),
        grid=(samples,),
        in_specs=[
            out,
            cache,
            cache,
            fresh,
            fresh,
            pl.BlockSpec(memory_space=pltpu.SMEM),
        ],
        out_specs=[out, out],
        out_shape=[jax.ShapeDtypeStruct((samples, rows, head_dim), F32)] * 2,
        compiler_params=pltpu.CompilerParams(vmem_limit_bytes=VMEM_BYTES),
        cost_estimate=pl.CostEstimate(
            flops=4 * samples * rows * flat * head_dim,
            bytes_accessed=4 * samples * flat * head_dim,
            transcendentals=samples * rows * flat,
        ),
        name="suffix",
    )(q, keys, values, new_keys, new_values, lengths)


def merge_kernel(sources, groups, samples, got_ref, own_ref, own_level_ref, out_ref):
    head_dim = own_ref.shape[2]
    per_sample = own_ref.shape[1] // groups
    per_dest = samples * per_sample
    for g in range(groups):
        levels, sizes = [], []
        for z in range(sources):
            packed = got_ref[z * groups + g, per_dest : per_dest + STAT_ROWS, :].astype(F32)
            parts = [[], []]
            for part in range(per_dest // STAT_ROWS):
                at = [
                    jnp.broadcast_to(packed[:, part * 8 + n : part * 8 + n + 1], (STAT_ROWS, head_dim))
                    for n in range(4)
                ]
                parts[0].append(at[0] + at[1] + at[2])
                parts[1].append(at[3] * (1.0 / CODE_SPAN))
            levels.append(jnp.concatenate(parts[0], axis=0))
            sizes.append(jnp.concatenate(parts[1], axis=0))
        for s in range(samples):
            own_level = own_level_ref[s, g * per_sample : (g + 1) * per_sample, :]
            highest = own_level
            here = slice(s * per_sample, (s + 1) * per_sample)
            for level in levels:
                highest = jnp.maximum(highest, level[here])
            weight = jnp.exp2(own_level - highest)
            total = weight
            summed = weight * own_ref[s, g * per_sample : (g + 1) * per_sample, :]
            for z in range(sources):
                coded = got_ref[z * groups + g, here, :].astype(F32)
                weight = jnp.exp2(levels[z][here] - highest)
                total = total + weight
                summed = summed + weight * (jnp.log2(coded) * sizes[z][here])
            result = summed / total
            out_ref[s, g * per_sample : (g + 1) * per_sample, :] = result.astype(BF16)


def merge_call(got, own, own_level, sources, groups):
    return pl.pallas_call(
        functools.partial(merge_kernel, sources, groups, own.shape[0]),
        out_shape=jax.ShapeDtypeStruct(own.shape, BF16),
        compiler_params=pltpu.CompilerParams(vmem_limit_bytes=VMEM_BYTES),
        name="merge",
    )(got, own, own_level)


def local(x_size, z_size, dec_size, queries, prompt_keys, prompt_values, suffix_keys, suffix_values, new_keys, new_values, lengths):
    samples, steps, width = queries.shape
    _, suffix_length, groups, head_dim = suffix_keys.shape
    per_group = width // (groups * head_dim)
    scale = head_dim ** (-0.5) * math.log2(math.e)
    keys = prompt_keys.reshape(-1, head_dim)
    values = prompt_values.reshape(-1, head_dim)

    def shift(array, amount):
        return lax.ppermute(array, "x", [(i, (i + amount) % x_size) for i in range(x_size)])

    keys_left, values_left = shift(keys, 1), shift(values, 1)
    keys_right, values_right = shift(keys, -1), shift(values, -1)
    keys_far, values_far = shift(keys_left, 1), shift(values_right, -1)

    per_dest = samples * steps * per_group
    per_sample = (
        queries.reshape(samples, steps, groups * per_group, head_dim)
        .transpose(0, 2, 1, 3)
        .reshape(samples, groups, per_group * steps, head_dim)
    )
    spread = jnp.broadcast_to(
        per_sample.transpose(1, 0, 2, 3)[None], (z_size, groups, samples, per_group * steps, head_dim)
    ).reshape(z_size * groups, per_dest, head_dim)
    rows = lax.all_to_all(spread, ("z", "dec"), 0, 0, tiled=True).reshape(-1, head_dim)

    own, own_level = suffix_call(
        per_sample.reshape(samples, groups * per_group * steps, head_dim),
        suffix_keys.reshape(samples, suffix_length * groups, head_dim),
        suffix_values.reshape(samples, suffix_length * groups, head_dim),
        new_keys.reshape(samples, steps * groups, head_dim),
        new_values.reshape(samples, steps * groups, head_dim),
        lengths,
        scale,
        groups,
        steps,
    )
    def prompt(some_keys, some_values, late, carry, final, sub):
        return prompt_call(rows, some_keys, some_values, late, carry, final, sub, 2048, scale, per_dest)

    carry = prompt([keys], [values], (), None, False, 256)
    coded = prompt(
        [keys_left, keys_right, keys_far], [values_left, values_right, values_far], (2, 5), carry, True, 128
    )
    got = lax.all_to_all(coded, ("z", "dec"), 0, 0, tiled=True)
    out = merge_call(got, own, own_level, z_size, groups)
    return (
        out.reshape(samples, groups * per_group, steps, head_dim)
        .transpose(0, 2, 1, 3)
        .reshape(samples, steps, width)
    )


def solution(mesh):
    ctx_size, dec_size = mesh.devices.shape
    x_size = 4
    z_size = ctx_size // x_size
    split = Mesh(mesh.devices.reshape(x_size, z_size, dec_size), ("x", "z", "dec"))
    rows = ("x", "z", "dec")
    return jax.shard_map(
        functools.partial(local, x_size, z_size, dec_size),
        mesh=split,
        in_specs=(
            P(rows, None, None),
            P(("x", "z"), "dec", None),
            P(("x", "z"), "dec", None),
            P(rows, None, None, None),
            P(rows, None, None, None),
            P(rows, None, None, None),
            P(rows, None, None, None),
            P(rows),
        ),
        out_specs=P(rows, None, None),
        check_vma=False,
    )
```
